256 devices in a mesh: clus: 16 (over z, core), sub: 16 (over y, x).
Axes of the slice: x: 4, y: 4, z: 8, core: 2. Of those that a mesh axis runs over, the one named last changes fastest.
Arguments:
- right_side: float32 [16, 16, 896, 512], P('clus', 'sub'), may hold values from -6 to 6
- dual_operator: float32 [16, 16, 896, 896], P('clus', 'sub'), may hold values from -1 to 3
- corner_basis: float32 [16, 16, 24, 896], P('clus', 'sub'), may hold values from -0.1875 to 0.1875
- coarse_inverse: float32 [16, 384, 384], P('clus'), may hold values from -1 to 2
- corner_map: int32 [16, 384], P('clus'), may hold values from 0 to 383, each once within a row
- iface_counts: int32 [16, 16, 16], P('clus', 'sub'), may hold values from 0 to 16, as said below
Outputs:
- solution: float32 [16, 16, 896, 512], P('clus', 'sub')
- residual: float32 [16, 16, 896, 512], P('clus', 'sub')
The draws below stay inside these ranges and needn't reach their ends.
Inputs may be any that keep to these rules, and one draw needn't show every extreme that they name: `iface_counts`: symmetric in its last two dimensions with a zero diagonal; in every cluster one subdomain shares exactly 16 multipliers with every other subdomain of the cluster.
All inputs are finite; a program needn't handle non-finite values.
Results may differ from the reference program's by a relative error of at most 0.00011.
Values sent between devices are 32-bit elements; how exact they have to be, the bound alone decides.
No kernel may reach another device: no remote copies, remote signals or barrier semaphores. Data moves between devices by JAX's collectives and lax.ppermute only.
A program may use at most 64 MiB of HBM per device.

```python
import math
import jax
import jax.numpy as jnp
from jax import lax

LOC = 896
NCOR = 24
XC = 128
CAP = 16
RHS = 512
ITERS = 3
CLUSTERS = 16
SUBS = 16
COARSE = 384


def draw_dual_operator(key, part):
    keys = jax.random.split(key, CLUSTERS * SUBS)

    def single(one_key):
        key_raw, key_diag, key_stiff = jax.random.split(one_key, 3)
        raw = jax.random.normal(key_raw, (LOC, LOC), jnp.float32)
        symmetric = (raw + raw.T) * (0.4 / math.sqrt(2.0 * LOC))
        diagonal = jax.random.uniform(key_diag, (LOC,), jnp.float32, 0.7, 1.3)
        stiffness = jnp.exp(jax.random.uniform(key_stiff, (), jnp.float32, math.log(0.5), math.log(2.0)))
        return (symmetric + jnp.diag(diagonal)) * stiffness
    return lax.map(single, keys).reshape(CLUSTERS, SUBS, LOC, LOC)


def draw_coarse_inverse(key, part):
    keys = jax.random.split(key, CLUSTERS)

    def single(one_key):
        raw = jax.random.normal(one_key, (COARSE, COARSE), jnp.float32)
        return jnp.eye(COARSE, dtype=jnp.float32) + raw * (0.8 / math.sqrt(COARSE))
    return lax.map(single, keys)


def draw_iface_counts(key, part):
    key_raw, key_star = jax.random.split(jax.random.fold_in(key, 7))
    raw = jax.random.randint(key_raw, (CLUSTERS, SUBS, SUBS), 0, CAP + 1)
    row_ids = jnp.arange(SUBS, dtype=jnp.int32)[:, None]
    col_ids = jnp.arange(SUBS, dtype=jnp.int32)[None, :]
    upper = jnp.where(col_ids > row_ids, raw, 0)
    symmetric = upper + jnp.swapaxes(upper, 1, 2)
    star = jax.random.randint(key_star, (CLUSTERS, 1, 1), 0, SUBS)
    touch = (row_ids[None] == star) | (col_ids[None] == star)
    result = jnp.where(touch, CAP, symmetric)
    result = jnp.where(row_ids[None] == col_ids[None], 0, result)
    return result.astype(jnp.int32)


def block_levels(key, dims, cuts, smallest, largest):
    def one(axis_at, shards_of):
        heights = jax.random.uniform(jax.random.fold_in(jax.random.fold_in(key, 6), axis_at), (shards_of,), jnp.float32, smallest / len(cuts), largest / len(cuts))
        return jnp.repeat(jnp.exp(heights), dims[axis_at] // shards_of).reshape((-1,) + (1,) * (len(dims) - axis_at - 1))

    level = one(*cuts[0])
    for cut in cuts[1:]:
        level = level * one(*cut)
    return level


def noise(stream_key, extent, scale, bound, cuts=(), kind=jnp.bfloat16):
    level = block_levels(stream_key, extent, cuts, -0.22, 0.18) if cuts else 1.0
    array = jax.random.normal(stream_key, extent, jnp.float32) * scale * level
    return jnp.minimum(jnp.maximum(array, -bound), bound).astype(kind)


def setup_inputs(seed: int = 0) -> dict:
    key_list = jax.random.split(jax.random.key(seed), 7)
    right_side = noise(key_list[0], (CLUSTERS, SUBS, LOC, RHS), 1.0, 6.0, ((0, 16), (1, 16)), jnp.float32)
    dual_operator = draw_dual_operator(jax.random.fold_in(key_list[6], 71), 0)
    corner_basis = noise(key_list[2], (CLUSTERS, SUBS, NCOR, LOC), LOC ** -0.5, 0.1875, ((0, 16), (1, 16)), jnp.float32)
    coarse_inverse = draw_coarse_inverse(jax.random.fold_in(key_list[6], 71), 0)
    corner_map = jax.vmap(lambda own: jax.random.permutation(own, COARSE))(jax.random.split(key_list[4], CLUSTERS)).reshape((CLUSTERS, COARSE)).astype(jnp.int32)
    iface_counts = draw_iface_counts(jax.random.fold_in(key_list[6], 71), 0)
    return {"right_side": right_side, "dual_operator": dual_operator, "corner_basis": corner_basis, "coarse_inverse": coarse_inverse, "corner_map": corner_map, "iface_counts": iface_counts}


spectrum_low = 0.5
spectrum_high = 3.0
center_value = (spectrum_high + spectrum_low) / 2.0
half_width = (spectrum_high - spectrum_low) / 2.0
sigma_one = center_value / half_width


def partner_rows(product, counts):
    finish = jnp.cumsum(counts, axis=2).astype(jnp.int32)
    starts = (finish - counts).astype(jnp.int32)
    position = (jnp.arange(LOC, dtype=jnp.int32) - 2 * XC)[None, None, :]
    source = jnp.sum((position[:, :, :, None] >= finish[:, :, None, :]).astype(jnp.int32), axis=3)
    usable = (position >= 0) & (source < SUBS)
    source = jnp.minimum(source, SUBS - 1).astype(jnp.int32)
    within = position - jnp.take_along_axis(starts, source, axis=2)
    theirs = jnp.take_along_axis(jnp.swapaxes(starts, 1, 2), source, axis=2)
    flat_index = jnp.where(usable, source * LOC + 2 * XC + theirs + within, 0).astype(jnp.int32)
    flat = product.reshape(CLUSTERS, SUBS * LOC, RHS)

    def pick(table, indices):
        return jnp.take(table, indices.reshape(-1), axis=0)

    inner = jax.vmap(pick)(flat, flat_index).reshape(CLUSTERS, SUBS, LOC, RHS)
    inner = jnp.where(usable[..., None], inner, jnp.zeros_like(inner))
    zeros = jnp.zeros((1, SUBS, XC, RHS), product.dtype)
    below = jnp.concatenate([zeros, product[:-1, :, XC:2 * XC]], axis=0)
    above = jnp.concatenate([product[1:, :, :XC], zeros], axis=0)
    return jnp.concatenate([below, above, inner[:, :, 2 * XC:]], axis=2)


def operator_apply(direction, dual_operator, corner_basis, coarse_inverse, corner_map, iface_counts):
    highest = lax.Precision.HIGHEST
    product = jnp.einsum('csij,csjr->csir', dual_operator, direction, precision=highest)
    assembled = product - partner_rows(product, iface_counts)
    corner_vals = jnp.einsum('csnl,cslr->csnr', corner_basis, direction, precision=highest)
    corner_vals = corner_vals.reshape(CLUSTERS, COARSE, RHS)

    def place(values, mapping):
        return jnp.zeros_like(values).at[mapping].set(values)

    coarse_rhs = jax.vmap(place)(corner_vals, corner_map)
    coarse_sol = jnp.einsum('cij,cjr->cir', coarse_inverse, coarse_rhs, precision=highest)
    back = jnp.take_along_axis(coarse_sol, corner_map[:, :, None].astype(jnp.int32), axis=1)
    back = back.reshape(CLUSTERS, SUBS, NCOR, RHS)
    return assembled + jnp.einsum('csnl,csnr->cslr', corner_basis, back, precision=highest)


def reference(right_side, dual_operator, corner_basis, coarse_inverse, corner_map, iface_counts):
    solution = jnp.zeros_like(right_side)
    residual = right_side
    ratio_now = 1.0 / sigma_one
    direction = right_side / center_value
    for iteration in range(ITERS):
        solution = solution + direction
        residual = residual - operator_apply(direction, dual_operator, corner_basis, coarse_inverse, corner_map, iface_counts)
        if iteration + 1 < ITERS:
            ratio_next = 1.0 / (2.0 * sigma_one - ratio_now)
            direction = (ratio_next * ratio_now) * direction + (2.0 * ratio_next / half_width) * residual
            ratio_now = ratio_next
    return solution, residual
```

```python
import jax
import jax.numpy as jnp
from jax import lax
from jax.experimental import pallas as pl
from jax.experimental.pallas import tpu as pltpu
from jax.sharding import PartitionSpec as P

LOC = 896
NCOR = 24
NPAD = 32
XC = 128
FACE = 2 * XC
CAP = 16
SUBS = 16
MID = SUBS * CAP
SPAN = CAP + 8
ITERS = 3
COARSE = SUBS * NCOR
ROWS = CAP + NCOR
WIDE = 256

spectrum_low = 0.5
spectrum_high = 3.0
center_value = (spectrum_high + spectrum_low) / 2.0
half_width = (spectrum_high - spectrum_low) / 2.0
sigma_one = center_value / half_width

BF = jnp.bfloat16
F32 = jnp.float32
SM = pl.BlockSpec(memory_space=pltpu.SMEM)
ANY = pl.BlockSpec(memory_space=pl.ANY)
VM = pl.BlockSpec(memory_space=pltpu.VMEM)


def split(x):
    hi = x.astype(BF)
    return hi, (x - hi.astype(F32)).astype(BF)


def mm(a, b):
    return jnp.dot(a, b, preferred_element_type=F32)


def mm3(ahi, alo, bhi, blo):
    return mm(ahi, bhi) + (mm(ahi, blo) + mm(alo, bhi))


def sds(shape, dtype=F32):
    return jax.ShapeDtypeStruct(shape, dtype)


def call(body, outs, ins, specs, scratch, copies, flops):
    return pl.pallas_call(
        body,
        out_shape=outs,
        in_specs=specs,
        out_specs=tuple(ANY for _ in outs),
        scratch_shapes=tuple(pltpu.VMEM(*s) for s in scratch) + (pltpu.SemaphoreType.DMA((copies,)),),
        compiler_params=pltpu.CompilerParams(vmem_limit_bytes=56 * 1024 * 1024),
        cost_estimate=pl.CostEstimate(flops=flops, bytes_accessed=6_000_000, transcendentals=0),
    )(*ins)


class Copies:
    def __init__(self, sems):
        self.sems, self.used, self.open = sems, 0, []

    def get(self, source, target):
        copy = pltpu.make_async_copy(source, target, self.sems.at[self.used])
        self.used += 1
        copy.start()
        return copy

    def put(self, source, target):
        self.open.append(self.get(source, target))

    def finish(self):
        for copy in self.open:
            copy.wait()


def face_starts(counts):
    starts, at = [], 0
    for p in range(SUBS):
        starts.append(at)
        at = at + counts[0, p]
    return starts, at


def place(at):
    low = lax.rem(at, 8)
    return pl.ds(pl.multiple_of(at - low, 8), SPAN), low


def take_rows(source, at):
    if isinstance(at, int):
        return source[at : at + CAP]
    window, low = place(at)
    return pltpu.roll(source[window, :], lax.rem(SPAN - low, SPAN), 0)[:CAP]


def put_rows(target, at, rows):
    if isinstance(at, int):
        target[at : at + CAP] = rows
        return
    window, low = place(at)
    moved = pltpu.roll(jnp.concatenate([rows, rows[:8]], axis=0), low, 0)
    keep = lax.broadcasted_iota(jnp.int32, moved.shape, 0) >= low
    target[window, :] = jnp.where(keep, moved, target[window, :])


def columns(width):
    return [pl.ds(at, WIDE) for at in range(0, width, WIDE)]


def fill(out, cols, product):
    for p in range(SUBS):
        out[p, :CAP, cols] = product[p * CAP : (p + 1) * CAP]
        out[p, CAP:, cols] = product[MID : MID + NCOR]


def padded(basis):
    return jnp.concatenate([basis, jnp.zeros((NPAD - NCOR, basis.shape[1]), F32)], axis=0)


def even_cluster():
    return lax.rem(lax.axis_index("clus"), 2) == 0


def pick(near, far):
    even = even_cluster()
    return jnp.where(even, far, near), jnp.where(even, near, far)


def sent_rows(flow, blocks, mhi_v, mlo_v, ends_v, dhi_v, dlo_v, out, near, far, out_v, near_v, far_v, prepare):
    for at, cols in enumerate(blocks):
        prepare(at, cols)
        fill(out_v, cols, mm3(mhi_v[...], mlo_v[...], dhi_v[:, cols], dlo_v[:, cols]))
        flow.put(out_v.at[:, :, cols], out.at[:, :, cols])
    prepare(len(blocks), None)
    zhi, zlo = split(ends_v[...])
    for cols in blocks:
        product = mm3(zhi, zlo, dhi_v[:, cols], dlo_v[:, cols])
        far_v[:, cols], near_v[:, cols] = pick(product[XC:], product[:XC])
        flow.put(far_v.at[:, cols], far.at[:, cols])
        flow.put(near_v.at[:, cols], near.at[:, cols])
    flow.finish()


def first_body(rhs, op, basis, counts, out, near, far, mhi, mlo, rhs_v, held, ends_v, basis_v, out_v, near_v, far_v, mhi_v, mlo_v, dhi_v, dlo_v, sems):
    flow = Copies(sems)
    rows_in = flow.get(op.at[pl.ds(FACE, MID + 8)], held)
    basis_in = flow.get(basis, basis_v)
    blocks = columns(rhs.shape[1])
    rhs_in = [flow.get(rhs.at[:, cols], rhs_v.at[:, cols]) for cols in blocks]
    ends_in = flow.get(op.at[pl.ds(0, FACE)], ends_v)
    basis_in.wait()
    mhi_v[MID:], mlo_v[MID:] = split(padded(basis_v[...]))
    starts, _ = face_starts(counts)
    rows_in.wait()
    for p in range(SUBS):
        rows = slice(p * CAP, (p + 1) * CAP)
        mhi_v[rows], mlo_v[rows] = split(take_rows(held, starts[p]))
    flow.put(mhi_v, mhi)
    flow.put(mlo_v, mlo)

    def prepare(at, cols):
        if cols is None:
            ends_in.wait()
        else:
            rhs_in[at].wait()
            dhi_v[:, cols], dlo_v[:, cols] = split(rhs_v[:, cols] * (1.0 / center_value))

    sent_rows(flow, blocks, mhi_v, mlo_v, ends_v, dhi_v, dlo_v, out, near, far, out_v, near_v, far_v, prepare)


def landed_body(near_in, far_in, edge, sems):
    flow = Copies(sems)
    even = even_cluster()
    near_at = pl.multiple_of(jnp.where(even, XC, 0), XC)
    far_at = pl.multiple_of(jnp.where(even, 0, XC), XC)
    flow.put(near_in, edge.at[pl.ds(near_at, XC)])
    flow.put(far_in, edge.at[pl.ds(far_at, XC)])
    flow.finish()


def table_rows(inverse_v, places, place_v, rows):
    own = lax.axis_index("sub") * NCOR
    rows[NCOR:] = jnp.zeros((NPAD - NCOR, COARSE), F32)
    for n in range(NCOR):
        rows[n : n + 1] = inverse_v[pl.ds(places[0, own + n], 1), :]
    chosen = lax.broadcasted_iota(jnp.int32, (COARSE, COARSE), 0) == place_v[...]
    chosen = jnp.where(chosen, 1.0, 0.0).astype(BF)
    top, mid = split(rows[...])
    low = (rows[...] - top.astype(F32) - mid.astype(F32)).astype(BF)
    return mm(top, chosen) + (mm(mid, chosen) + mm(low, chosen))


def table_body(inverse, places, place_row, basis, table, turned, inverse_v, place_v, basis_v, rows, table_v, turned_v, sems):
    flow = Copies(sems)
    inverse_in = [flow.get(inverse, inverse_v), flow.get(place_row, place_v)]
    basis_in = flow.get(basis, basis_v)
    for copy in inverse_in:
        copy.wait()
    table_v[:NPAD], table_v[NPAD:] = split(table_rows(inverse_v, places, place_v, rows))
    flow.put(table_v, table)
    basis_in.wait()
    bhi, blo = split(padded(basis_v[...]).T)
    turned_v[...] = jnp.concatenate([bhi, bhi, blo], axis=1)
    flow.put(turned_v, turned)
    flow.finish()


HALF = (LOC - FACE) // 2
CHUNKS = (pl.ds(FACE, HALF), pl.ds(FACE + HALF, HALF))


def rest_body(in_scale, new_by, old_by, product_by, last):
    olds = 0 if old_by is None else 2 if last else 1

    def body(op, near, far, dirn, *refs):
        before, refs = refs[:olds], refs[olds:]
        outs, refs = refs[: 1 + last], refs[1 + last :]
        (op_v, near_v, far_v, dirn_v), refs = refs[:4], refs[4:]
        before_v, made, sems = refs[:olds], refs[olds:-1], refs[-1]
        flow = Copies(sems)
        blocks = columns(dirn.shape[1])
        op_in, dirn_in, before_in = [], [], []
        for at, cols in enumerate(blocks):
            dirn_in.append(flow.get(dirn.at[:, cols], dirn_v.at[:, cols]))
            if at == 0:
                op_in.append(flow.get(op.at[CHUNKS[0]], op_v.at[CHUNKS[0]]))
            before_in.append([flow.get(x.at[:, cols], y.at[:, cols]) for x, y in zip(before, before_v)])
            if at == 0:
                op_in.append(flow.get(op.at[CHUNKS[1]], op_v.at[CHUNKS[1]]))
                edges_in = [flow.get(near, near_v), flow.get(far, far_v)]
        factors = []
        for at, cols in enumerate(blocks):
            dirn_in[at].wait()
            dhi, dlo = split(dirn_v[:, cols] * in_scale)

            def store(rows, product):
                value = new_by * dirn_v[rows, cols] - product_by * product
                if olds:
                    value = value + old_by * before_v[0][rows, cols]
                made[0][rows, cols] = value
                flow.put(made[0].at[rows, cols], outs[0].at[rows, cols])

            for part, rows in enumerate(CHUNKS):
                if at == 0:
                    op_in[part].wait()
                    factors.append(split(op_v[rows]))
                if part == 0:
                    for copy in before_in[at]:
                        copy.wait()
                store(rows, mm3(*factors[part], dhi, dlo))
            if at == 0:
                for copy in edges_in:
                    copy.wait()
            low, high = pick(near_v[:, cols], far_v[:, cols])
            store(pl.ds(0, FACE), jnp.concatenate([low, high], axis=0))
            if last:
                made[1][:, cols] = before_v[1][:, cols] * (1.0 / center_value) + before_v[0][:, cols] + dirn_v[:, cols]
                flow.put(made[1].at[:, cols], outs[1].at[:, cols])
        flow.finish()

    return body


def change(cols, arrived, table, turned, starts, total, inner, waits):
    for p in range(SUBS):
        put_rows(inner, starts[p], arrived[p, :CAP, cols])
    usable = lax.broadcasted_iota(jnp.int32, (MID, WIDE), 0) < total
    faces = jnp.where(usable, inner[:MID], 0.0)
    pieces = jnp.concatenate([arrived[p, CAP:, cols] for p in range(SUBS)], axis=0)
    phi, plo = split(pieces)
    for copy in waits:
        copy.wait()
    both = mm(table[...], phi)
    back = both[:NPAD] + (both[NPAD:] + mm(table[:NPAD], plo))
    yhi, ylo = split(back)
    return mm(turned[...], jnp.concatenate([yhi, ylo, yhi], axis=0)), faces


def update(cols, source, edge, fix, faces, scale, store):
    rows = slice(0, FACE)
    store(rows, source[rows, cols] + scale * (edge[:, cols] - fix[rows]))
    rows = slice(FACE, FACE + MID)
    store(rows, source[rows, cols] + scale * (faces - fix[rows]))
    rows = slice(FACE + MID, LOC)
    store(rows, source[rows, cols] - scale * fix[rows])


def next_body(scale_r):
    def body(
        arrived, base, edge, table, turned, mhi, mlo, op, counts, out, near, far, dirn,
        base_v, edge_v, table_v, turned_v, mhi_v, mlo_v, ends_v, out_v, near_v, far_v, dirn_v, dhi_v, dlo_v, inner, sems,
    ):
        flow = Copies(sems)
        starts, total = face_starts(counts)
        blocks = columns(base.shape[1])
        table_in = [flow.get(table, table_v), flow.get(turned, turned_v)]
        base_in = [[flow.get(base.at[:, blocks[0]], base_v.at[:, blocks[0]]), flow.get(edge, edge_v)]]
        m_in = [flow.get(mhi, mhi_v), flow.get(mlo, mlo_v)]
        base_in += [[flow.get(base.at[:, cols], base_v.at[:, cols])] for cols in blocks[1:]]
        ends_in = flow.get(op.at[pl.ds(0, FACE)], ends_v)

        def prepare(at, cols):
            if cols is None:
                ends_in.wait()
                return
            fix, faces = change(cols, arrived, table_v, turned_v, starts, total, inner, table_in if at == 0 else ())
            for copy in base_in[at]:
                copy.wait()

            def store(rows, value):
                dirn_v[rows, cols] = value
                dhi_v[rows, cols], dlo_v[rows, cols] = split(value)

            update(cols, base_v, edge_v, fix, faces, scale_r, store)
            flow.put(dirn_v.at[:, cols], dirn.at[:, cols])
            if at == 0:
                for copy in m_in:
                    copy.wait()

        sent_rows(flow, blocks, mhi_v, mlo_v, ends_v, dhi_v, dlo_v, out, near, far, out_v, near_v, far_v, prepare)

    return body


def last_body(arrived, left, edge, table, turned, counts, res, left_v, edge_v, table_v, turned_v, res_v, inner, sems):
    flow = Copies(sems)
    starts, total = face_starts(counts)
    blocks = columns(left.shape[1])
    table_in = [flow.get(table, table_v), flow.get(turned, turned_v)]
    edge_in = flow.get(edge, edge_v)
    left_in = [flow.get(left.at[:, cols], left_v.at[:, cols]) for cols in blocks]
    for at, cols in enumerate(blocks):
        fix, faces = change(cols, arrived, table_v, turned_v, starts, total, inner, table_in if at == 0 else ())
        if at == 0:
            edge_in.wait()
        left_in[at].wait()

        def store(rows, value):
            res_v[rows, cols] = value

        update(cols, left_v, edge_v, fix, faces, 1.0, store)
        flow.put(res_v.at[:, cols], res.at[:, cols])
    flow.finish()


def pairs(first, count):
    route = []
    for low in range(first, count - 1, 2):
        route += [(low, low + 1), (low + 1, low)]
    return route


def scales():
    found, ratio = [], 1.0 / sigma_one
    for _ in range(ITERS - 1):
        ratio_next = 1.0 / (2.0 * sigma_one - ratio)
        found.append((ratio_next * ratio, 2.0 * ratio_next / half_width))
        ratio = ratio_next
    return found


def on_device(right_side, dual_operator, corner_basis, coarse_inverse, corner_map, iface_counts):
    rhs = right_side[0, 0]
    op = dual_operator[0, 0]
    basis = corner_basis[0, 0]
    inverse = coarse_inverse[0]
    counts = iface_counts[0]
    width = rhs.shape[1]
    clusters = lax.axis_size("clus")
    state, edge, sent = (LOC, width), (XC, width), (SUBS, ROWS, width)
    mids, ends = (MID + NPAD, LOC), (FACE, LOC)
    tables, turns, held = (2 * NPAD, COARSE), (LOC, 3 * NPAD), (MID + 8, WIDE)
    steps = scales()

    def exchange(out):
        return lax.all_to_all(out, "sub", split_axis=0, concat_axis=0, tiled=True)

    def swap(near, far):
        far = lax.ppermute(far, "clus", pairs(1, clusters))
        return lax.ppermute(near, "clus", pairs(0, clusters)), far

    def landed(near_in, far_in):
        return call(landed_body, (sds((FACE, width)),), (near_in, far_in), (VM, VM), (), 2, 1_000_000)[0]

    def rest(body, near, far, dirn, before, last):
        return call(
            body,
            (sds(state),) * (1 + last),
            (op, near, far, dirn) + before,
            (ANY,) * (4 + len(before)),
            (((LOC, LOC), F32), (edge, F32), (edge, F32)) + ((state, F32),) * (2 + last + len(before)),
            20,
            2_000_000_000,
        )

    out, near, far, mhi, mlo = call(
        first_body,
        (sds(sent), sds(edge), sds(edge), sds(mids, BF), sds(mids, BF)),
        (rhs, op, basis, counts),
        (ANY, ANY, ANY, SM),
        ((state, F32), ((MID + 8, LOC), F32), (ends, F32), ((NCOR, LOC), F32), (sent, F32), (edge, F32), (edge, F32), (mids, BF), (mids, BF), (state, BF), (state, BF)),
        14,
        800_000_000,
    )
    arrived = exchange(out)
    near_in, far_in = swap(near, far)
    scale_d, scale_r = steps[0]
    inverse_center = 1.0 / center_value
    made = rest(rest_body(inverse_center, scale_d * inverse_center + scale_r, None, scale_r, False), near, far, rhs, (), False)
    table, turned = call(
        table_body,
        (sds(tables, BF), sds(turns, BF)),
        (inverse, corner_map, corner_map, basis),
        (ANY, SM, ANY, ANY),
        (((COARSE, COARSE), F32), ((1, COARSE), jnp.int32), ((NCOR, LOC), F32), ((NPAD, COARSE), F32), (tables, BF), (turns, BF)),
        5,
        200_000_000,
    )
    landing = landed(near_in, far_in)
    before = (rhs,)
    for at in range(1, ITERS):
        last = at == ITERS - 1
        back_d, back_r = steps[at - 1]
        out, near, far, dirn = call(
            next_body(back_r),
            (sds(sent), sds(edge), sds(edge), sds(state)),
            (arrived, made[0], landing, table, turned, mhi, mlo, op, counts),
            (VM,) + (ANY,) * 7 + (SM,),
            ((state, F32), ((FACE, width), F32), (tables, BF), (turns, BF), (mids, BF), (mids, BF), (ends, F32), (sent, F32), (edge, F32), (edge, F32),
             (state, F32), (state, BF), (state, BF), (held, F32)),
            18,
            1_000_000_000,
        )
        arrived = exchange(out)
        near_in, far_in = swap(near, far)
        old_by = -back_d / back_r * (inverse_center if at == 1 else 1.0)
        new_by, product_by = 1.0 / back_r, 1.0
        if not last:
            scale_d, scale_r = steps[at]
            new_by, old_by, product_by = scale_d + scale_r * new_by, scale_r * old_by, scale_r
        made = rest(rest_body(1.0, new_by, old_by, product_by, last), near, far, dirn, before, last)
        landing = landed(near_in, far_in)
        before = (dirn,) + before
    (res,) = call(
        last_body,
        (sds(state),),
        (arrived, made[0], landing, table, turned, counts),
        (VM,) + (ANY,) * 4 + (SM,),
        ((state, F32), ((FACE, width), F32), (tables, BF), (turns, BF), (state, F32), (held, F32)),
        8,
        100_000_000,
    )
    return (made[1][None, None], res[None, None])


def solution(mesh):
    placed = (
        P("clus", "sub", None, None),
        P("clus", "sub", None, None),
        P("clus", "sub", None, None),
        P("clus", None, None),
        P("clus", None),
        P("clus", "sub", None),
    )
    return jax.shard_map(
        on_device,
        mesh=mesh,
        in_specs=placed,
        out_specs=(P("clus", "sub", None, None), P("clus", "sub", None, None)),
        check_vma=False,
    )
```

```python
import jax
import jax.numpy as jnp
from jax import lax
from jax.experimental import pallas as pl
from jax.experimental.pallas import tpu as pltpu
from jax.sharding import PartitionSpec as P

LOC = 896
NCOR = 24
NPAD = 32
XC = 128
FACE = 2 * XC
CAP = 16
SUBS = 16
MID = SUBS * CAP
BORDER = FACE + MID
SPAN = CAP + 8
ITERS = 3
COARSE = SUBS * NCOR
ROWS = CAP + NCOR
WIDE = 256

spectrum_low = 0.5
spectrum_high = 3.0
center_value = (spectrum_high + spectrum_low) / 2.0
half_width = (spectrum_high - spectrum_low) / 2.0
sigma_one = center_value / half_width

WINDOW_GRANT, CRITICAL_GRANT, FIRST_GRANT = 52, 51, 59
BF = jnp.bfloat16
F32 = jnp.float32
SM = pl.BlockSpec(memory_space=pltpu.SMEM)
ANY = pl.BlockSpec(memory_space=pl.ANY)
VM = pl.BlockSpec(memory_space=pltpu.VMEM)


def split(x):
    hi = x.astype(BF)
    return hi, (x - hi.astype(F32)).astype(BF)


def mm(a, b):
    return jnp.dot(a, b, preferred_element_type=F32)


def mm3(ahi, alo, bhi, blo):
    return mm(ahi, bhi) + (mm(ahi, blo) + mm(alo, bhi))


def sds(shape, dtype=F32):
    return jax.ShapeDtypeStruct(shape, dtype)


def call(body, outs, ins, specs, scratch, copies, flops, grant=WINDOW_GRANT):
    return pl.pallas_call(
        body,
        out_shape=outs,
        in_specs=specs,
        out_specs=tuple(ANY for _ in outs),
        scratch_shapes=tuple(pltpu.VMEM(*s) for s in scratch) + (pltpu.SemaphoreType.DMA((copies,)),),
        compiler_params=pltpu.CompilerParams(vmem_limit_bytes=grant * 1024 * 1024),
        cost_estimate=pl.CostEstimate(flops=flops, bytes_accessed=6_000_000, transcendentals=0),
    )(*ins)


class Copies:
    def __init__(self, sems):
        self.sems, self.used, self.open = sems, 0, []

    def get(self, source, target):
        copy = pltpu.make_async_copy(source, target, self.sems.at[self.used])
        self.used += 1
        copy.start()
        return copy

    def put(self, source, target):
        self.open.append(self.get(source, target))

    def finish(self):
        for copy in self.open:
            copy.wait()


def face_starts(counts):
    starts, at = [], 0
    for p in range(SUBS):
        starts.append(at)
        at = at + counts[0, p]
    return starts, at


def place(at):
    low = lax.rem(at, 8)
    return pl.ds(pl.multiple_of(at - low, 8), SPAN), low


def take_rows(source, at):
    if isinstance(at, int):
        return source[at : at + CAP]
    window, low = place(at)
    return pltpu.roll(source[window, :], lax.rem(SPAN - low, SPAN), 0)[:CAP]


def put_rows(target, at, rows):
    if isinstance(at, int):
        target[at : at + CAP] = rows
        return
    window, low = place(at)
    moved = pltpu.roll(jnp.concatenate([rows, rows[:8]], axis=0), low, 0)
    keep = lax.broadcasted_iota(jnp.int32, moved.shape, 0) >= low
    target[window, :] = jnp.where(keep, moved, target[window, :])


def columns(width):
    return [pl.ds(at, WIDE) for at in range(0, width, WIDE)]


def fill(out, cols, product):
    for p in range(SUBS):
        out[p, :CAP, cols] = product[p * CAP : (p + 1) * CAP]
        out[p, CAP:, cols] = product[MID : MID + NCOR]


def padded(basis):
    return jnp.concatenate([basis, jnp.zeros((NPAD - NCOR, basis.shape[1]), F32)], axis=0)


def even_cluster():
    return lax.rem(lax.axis_index("clus"), 2) == 0


def pick(near, far):
    even = even_cluster()
    return jnp.where(even, far, near), jnp.where(even, near, far)


def first_body(rhs, op, basis, counts, out, mhe, mle, mhr, mlr, rhs_v, held, basis_v, out_v, mhi_v, mlo_v, sems):
    flow = Copies(sems)
    rows_in = flow.get(op.at[pl.ds(FACE, MID + 8)], held)
    basis_in = flow.get(basis, basis_v)
    blocks = columns(rhs.shape[1])
    rhs_in = [flow.get(rhs.at[:, cols], rhs_v.at[:, cols]) for cols in blocks]
    basis_in.wait()
    mhi_v[MID:], mlo_v[MID:] = split(padded(basis_v[...]))
    starts, _ = face_starts(counts)
    rows_in.wait()
    for p in range(SUBS):
        rows = slice(p * CAP, (p + 1) * CAP)
        mhi_v[rows], mlo_v[rows] = split(take_rows(held, starts[p]))
    for cols, ready in zip(blocks, rhs_in):
        ready.wait()
        dhi, dlo = split(rhs_v[:, cols] * (1.0 / center_value))
        fill(out_v, cols, mm3(mhi_v[...], mlo_v[...], dhi, dlo))
        flow.put(out_v.at[:, :, cols], out.at[:, :, cols])
    for source, near_face, others in ((mhi_v, mhe, mhr), (mlo_v, mle, mlr)):
        flow.put(source.at[:, pl.ds(0, BORDER)], near_face)
        flow.put(source.at[:, pl.ds(BORDER, LOC - BORDER)], others)
    flow.finish()


def edge_rows(flow, blocks, ends, direction, near, far, near_v, far_v):
    for at, cols in enumerate(blocks):
        dhi, dlo = split(direction(at, cols))
        if at == 0:
            zhi, zlo = split(ends())
        product = mm3(zhi, zlo, dhi, dlo)
        far_v[:, cols], near_v[:, cols] = pick(product[XC:], product[:XC])
        flow.put(far_v.at[:, cols], far.at[:, cols])
        flow.put(near_v.at[:, cols], near.at[:, cols])
    flow.finish()


def edge_first_body(rhs, op, near, far, rhs_v, ends_v, near_v, far_v, sems):
    flow = Copies(sems)
    blocks = columns(rhs.shape[1])
    ends_in = flow.get(op.at[pl.ds(0, FACE)], ends_v)
    rhs_in = [flow.get(rhs.at[:, cols], rhs_v.at[:, cols]) for cols in blocks]

    def ends():
        ends_in.wait()
        return ends_v[...]

    def direction(at, cols):
        rhs_in[at].wait()
        return rhs_v[:, cols] * (1.0 / center_value)

    edge_rows(flow, blocks, ends, direction, near, far, near_v, far_v)


def edge_body(scale_r):
    def body(part, small, base, turned, op, dirn, near, far, part_v, small_v, base_v, turned_v, ends_v, dirn_v, near_v, far_v, sems):
        flow = Copies(sems)
        blocks = columns(base.shape[1])
        first_in = [flow.get(turned, turned_v), flow.get(small, small_v)]
        block_in = [[flow.get(x.at[:, cols], y.at[:, cols]) for x, y in ((part, part_v), (base.at[pl.ds(0, LOC)], base_v))] for cols in blocks]
        ends_in = flow.get(op.at[pl.ds(0, FACE)], ends_v)

        def ends():
            ends_in.wait()
            return ends_v[...]

        def direction(at, cols):
            for copy in (first_in if at == 0 else []) + block_in[at]:
                copy.wait()
            fix = mm(turned_v[...], small_v[:, cols])
            top, rest = slice(0, BORDER), slice(BORDER, LOC)
            dirn_v[top, cols] = base_v[top, cols] + scale_r * (part_v[:, cols] - fix[top])
            dirn_v[rest, cols] = base_v[rest, cols] - scale_r * fix[rest]
            flow.put(dirn_v.at[:, cols], dirn.at[:, cols])
            return dirn_v[:, cols]

        edge_rows(flow, blocks, ends, direction, near, far, near_v, far_v)

    return body


def landed_body(near_in, far_in, edge, sems):
    flow = Copies(sems)
    even = even_cluster()
    near_at = pl.multiple_of(jnp.where(even, XC, 0), XC)
    far_at = pl.multiple_of(jnp.where(even, 0, XC), XC)
    flow.put(near_in, edge.at[pl.ds(near_at, XC)])
    flow.put(far_in, edge.at[pl.ds(far_at, XC)])
    flow.finish()


def table_rows(inverse_v, places, place_v, rows):
    own = lax.axis_index("sub") * NCOR
    rows[NCOR:] = jnp.zeros((NPAD - NCOR, COARSE), F32)
    for n in range(NCOR):
        rows[n : n + 1] = inverse_v[pl.ds(places[0, own + n], 1), :]
    chosen = lax.broadcasted_iota(jnp.int32, (COARSE, COARSE), 0) == place_v[...]
    chosen = jnp.where(chosen, 1.0, 0.0).astype(BF)
    top, mid = split(rows[...])
    low = (rows[...] - top.astype(F32) - mid.astype(F32)).astype(BF)
    return mm(top, chosen) + (mm(mid, chosen) + mm(low, chosen))


def m_copies(flow, parts, mhi_v, mlo_v):
    mhe, mle, mhr, mlr = parts
    top, rest = pl.ds(0, BORDER), pl.ds(BORDER, LOC - BORDER)
    pairs_in = ((mhe, mhi_v.at[:, top]), (mhr, mhi_v.at[:, rest]), (mle, mlo_v.at[:, top]), (mlr, mlo_v.at[:, rest]))
    return [flow.get(source, target) for source, target in pairs_in]


def table_body(inverse, places, place_row, basis, mhe, mle, mhr, mlr, table, turned, crossed, inverse_v, place_v, basis_v, rows, mhi_v, mlo_v, table_v, turned_v, crossed_v, sems):
    flow = Copies(sems)
    inverse_in = [flow.get(inverse, inverse_v), flow.get(place_row, place_v)]
    basis_in = flow.get(basis, basis_v)
    m_in = m_copies(flow, (mhe, mle, mhr, mlr), mhi_v, mlo_v)
    for copy in inverse_in:
        copy.wait()
    table_v[:NPAD], table_v[NPAD:] = split(table_rows(inverse_v, places, place_v, rows))
    flow.put(table_v, table)
    basis_in.wait()
    bhi, blo = split(padded(basis_v[...]).T)
    turned_v[...] = jnp.concatenate([bhi, bhi, blo], axis=1)
    flow.put(turned_v, turned)
    for copy in m_in:
        copy.wait()
    chi, clo = split(mm3(mhi_v[...], mlo_v[...], bhi, blo))
    crossed_v[...] = jnp.concatenate([chi, chi, clo], axis=1)
    flow.put(crossed_v, crossed)
    flow.finish()


AHEAD = pl.ds(LOC, MID + NPAD)
HALF = (LOC - FACE) // 2
CHUNKS = (pl.ds(FACE, HALF), pl.ds(FACE + HALF, HALF))


def rest_body(in_scale, new_by, old_by, product_by, last):
    olds = 0 if old_by is None else 2 if last else 1

    def body(op, near, far, dirn, *refs):
        before, refs = refs[:olds], refs[olds:]
        parts, refs = (refs[:4], refs[4:]) if not last else ((), refs)
        outs, refs = refs[: 1 + last], refs[1 + last :]
        (op_v, near_v, far_v, dirn_v), refs = refs[:4], refs[4:]
        before_v, refs = refs[:olds], refs[olds:]
        m_v, refs = (refs[:2], refs[2:]) if not last else ((), refs)
        made, sems = refs[:-1], refs[-1]
        flow = Copies(sems)
        blocks = columns(dirn.shape[1])
        op_in, dirn_in, before_in, m_in = [], [], [], []
        for at, cols in enumerate(blocks):
            dirn_in.append(flow.get(dirn.at[:, cols], dirn_v.at[:, cols]))
            if at == 0:
                op_in.append(flow.get(op.at[CHUNKS[0]], op_v.at[CHUNKS[0]]))
            before_in.append([flow.get(x.at[:, cols], y.at[:, cols]) for x, y in zip(before, before_v)])
            if at == 0:
                op_in.append(flow.get(op.at[CHUNKS[1]], op_v.at[CHUNKS[1]]))
                edges_in = [flow.get(near, near_v), flow.get(far, far_v)]
                m_in = [] if last else m_copies(flow, parts, *m_v)
        factors = []
        for at, cols in enumerate(blocks):
            dirn_in[at].wait()
            dhi, dlo = split(dirn_v[:, cols] * in_scale)

            def store(rows, product):
                value = new_by * dirn_v[rows, cols] - product_by * product
                if olds:
                    value = value + old_by * before_v[0][rows, cols]
                made[0][rows, cols] = value
                flow.put(made[0].at[rows, cols], outs[0].at[rows, cols])

            for part, rows in enumerate(CHUNKS):
                if at == 0:
                    op_in[part].wait()
                    factors.append(split(op_v[rows]))
                if part == 0:
                    for copy in before_in[at]:
                        copy.wait()
                store(rows, mm3(*factors[part], dhi, dlo))
            if at == 0:
                for copy in edges_in:
                    copy.wait()
            low, high = pick(near_v[:, cols], far_v[:, cols])
            store(pl.ds(0, FACE), jnp.concatenate([low, high], axis=0))
            if last:
                made[1][:, cols] = before_v[1][:, cols] * (1.0 / center_value) + before_v[0][:, cols] + dirn_v[:, cols]
                flow.put(made[1].at[:, cols], outs[1].at[:, cols])
            else:
                if at == 0:
                    for copy in m_in:
                        copy.wait()
                made[1][:, cols] = mm3(m_v[0][...], m_v[1][...], *split(made[0][:, cols]))
                flow.put(made[1].at[:, cols], outs[0].at[AHEAD, cols])
        flow.finish()

    return body


def arrived_faces(cols, arrived, starts, total, inner):
    for p in range(SUBS):
        put_rows(inner, starts[p], arrived[p, :CAP, cols])
    usable = lax.broadcasted_iota(jnp.int32, (MID, WIDE), 0) < total
    return jnp.where(usable, inner[:MID], 0.0)


def arrived_back(cols, arrived, table):
    pieces = jnp.concatenate([arrived[p, CAP:, cols] for p in range(SUBS)], axis=0)
    phi, plo = split(pieces)
    both = mm(table[...], phi)
    back = both[:NPAD] + (both[NPAD:] + mm(table[:NPAD], plo))
    yhi, ylo = split(back)
    return jnp.concatenate([yhi, ylo, yhi], axis=0)


def update(cols, source, edge, fix, faces, scale, store):
    rows = slice(0, FACE)
    store(rows, source[rows, cols] + scale * (edge[:, cols] - fix[rows]))
    rows = slice(FACE, FACE + MID)
    store(rows, source[rows, cols] + scale * (faces - fix[rows]))
    rows = slice(FACE + MID, LOC)
    store(rows, source[rows, cols] - scale * fix[rows])


def next_body(scale_r):
    def body(arrived, mhe, mle, table, crossed, ahead, edge, counts, out, part, small, ahead_v, part_v, small_v, out_v, inner, sems):
        flow = Copies(sems)
        edge_in = flow.get(edge, part_v.at[pl.ds(0, FACE)])
        ahead_in = flow.get(ahead.at[AHEAD], ahead_v)
        starts, total = face_starts(counts)
        blocks = columns(edge.shape[1])
        for at, cols in enumerate(blocks):
            back = arrived_back(cols, arrived, table)
            small_v[:, cols] = back
            part_v[FACE:, cols] = arrived_faces(cols, arrived, starts, total, inner)
            if at == 0:
                edge_in.wait()
            product = mm3(mhe[...], mle[...], *split(part_v[:, cols])) - mm(crossed[...], back)
            if at == 0:
                ahead_in.wait()
            fill(out_v, cols, ahead_v[:, cols] + scale_r * product)
            flow.put(out_v.at[:, :, cols], out.at[:, :, cols])
            flow.put(part_v.at[:, cols], part.at[:, cols])
        flow.put(small_v, small)
        flow.finish()

    return body


def last_body(arrived, left, edge, table, turned, counts, res, left_v, edge_v, table_v, turned_v, res_v, inner, sems):
    flow = Copies(sems)
    starts, total = face_starts(counts)
    blocks = columns(left.shape[1])
    table_in = [flow.get(table, table_v), flow.get(turned, turned_v)]
    edge_in = flow.get(edge, edge_v)
    left_in = [flow.get(left.at[:, cols], left_v.at[:, cols]) for cols in blocks]
    for at, cols in enumerate(blocks):
        faces = arrived_faces(cols, arrived, starts, total, inner)
        if at == 0:
            for copy in table_in:
                copy.wait()
        fix = mm(turned_v[...], arrived_back(cols, arrived, table_v))
        if at == 0:
            edge_in.wait()
        left_in[at].wait()

        def store(rows, value):
            res_v[rows, cols] = value

        update(cols, left_v, edge_v, fix, faces, 1.0, store)
        flow.put(res_v.at[:, cols], res.at[:, cols])
    flow.finish()


def pairs(first, count):
    route = []
    for low in range(first, count - 1, 2):
        route += [(low, low + 1), (low + 1, low)]
    return route


def scales():
    found, ratio = [], 1.0 / sigma_one
    for _ in range(ITERS - 1):
        ratio_next = 1.0 / (2.0 * sigma_one - ratio)
        found.append((ratio_next * ratio, 2.0 * ratio_next / half_width))
        ratio = ratio_next
    return found


def on_device(right_side, dual_operator, corner_basis, coarse_inverse, corner_map, iface_counts):
    rhs = right_side[0, 0]
    op = dual_operator[0, 0]
    basis = corner_basis[0, 0]
    inverse = coarse_inverse[0]
    counts = iface_counts[0]
    width = rhs.shape[1]
    clusters = lax.axis_size("clus")
    state, edge, sent = (LOC, width), (XC, width), (SUBS, ROWS, width)
    mids, ends = (MID + NPAD, LOC), (FACE, LOC)
    tables, turns, held = (2 * NPAD, COARSE), (LOC, 3 * NPAD), (MID + 8, WIDE)
    steps = scales()

    def exchange(out):
        return lax.all_to_all(out, "sub", split_axis=0, concat_axis=0, tiled=True)

    def swap(near, far):
        far = lax.ppermute(far, "clus", pairs(1, clusters))
        return lax.ppermute(near, "clus", pairs(0, clusters)), far

    def landed(near_in, far_in):
        return call(landed_body, (sds((FACE, width)),), (near_in, far_in), (VM, VM), (), 2, 1_000_000, WINDOW_GRANT)[0]

    border, others = (MID + NPAD, BORDER), (MID + NPAD, LOC - BORDER)
    crosses, ahead_s, part_s, small_s = (MID + NPAD, 3 * NPAD), (MID + NPAD, width), (BORDER, width), (3 * NPAD, width)
    inverse_center = 1.0 / center_value

    out, mhe, mle, mhr, mlr = call(
        first_body,
        (sds(sent), sds(border, BF), sds(border, BF), sds(others, BF), sds(others, BF)),
        (rhs, op, basis, counts),
        (ANY, ANY, ANY, SM),
        ((state, F32), ((MID + 8, LOC), F32), ((NCOR, LOC), F32), (sent, F32), (mids, BF), (mids, BF)),
        10,
        800_000_000,
        FIRST_GRANT,
    )
    parts = (mhe, mle, mhr, mlr)

    def rest(body, near, far, dirn, before, last):
        return call(
            body,
            (sds(state), sds(state)) if last else (sds((LOC + MID + NPAD, width)),),
            (op, near, far, dirn) + before + (() if last else parts),
            (ANY,) * (4 + len(before) + 4 * (not last)),
            (((LOC, LOC), F32), (edge, F32), (edge, F32), (state, F32)) + ((state, F32),) * len(before)
            + (() if last else ((mids, BF), (mids, BF))) + ((state, F32), (state if last else ahead_s, F32)),
            24,
            2_000_000_000,
            WINDOW_GRANT,
        )

    arrived = exchange(out)
    near, far = call(
        edge_first_body,
        (sds(edge), sds(edge)),
        (rhs, op),
        (ANY, ANY),
        ((state, F32), (ends, F32), (edge, F32), (edge, F32)),
        7,
        700_000_000,
    )
    near_in, far_in = swap(near, far)
    scale_d, scale_r = steps[0]
    made = rest(rest_body(inverse_center, scale_d * inverse_center + scale_r, None, scale_r, False), near, far, rhs, (), False)
    table, turned, crossed = call(
        table_body,
        (sds(tables, BF), sds(turns, BF), sds(crosses, BF)),
        (inverse, corner_map, corner_map, basis) + parts,
        (ANY, SM) + (ANY,) * 6,
        (((COARSE, COARSE), F32), ((1, COARSE), jnp.int32), ((NCOR, LOC), F32), ((NPAD, COARSE), F32), (mids, BF), (mids, BF),
         (tables, BF), (turns, BF), (crosses, BF)),
        10,
        200_000_000,
        WINDOW_GRANT,
    )
    landing = landed(near_in, far_in)
    before = (rhs,)
    for at in range(1, ITERS):
        last = at == ITERS - 1
        back_d, back_r = steps[at - 1]
        out, part, small = call(
            next_body(back_r),
            (sds(sent), sds(part_s), sds(small_s, BF)),
            (arrived, mhe, mle, table, crossed, made[0], landing, counts),
            (VM,) * 5 + (ANY,) * 2 + (SM,),
            ((ahead_s, F32), (part_s, F32), (small_s, BF), (sent, F32), (held, F32)),
            7,
            1_000_000_000,
            CRITICAL_GRANT,
        )
        arrived = exchange(out)
        dirn, near, far = call(
            edge_body(back_r),
            (sds(state), sds(edge), sds(edge)),
            (part, small, made[0], turned, op),
            (ANY,) * 5,
            ((part_s, F32), (small_s, BF), (state, F32), (turns, BF), (ends, F32), (state, F32), (edge, F32), (edge, F32)),
            13,
            700_000_000,
        )
        near_in, far_in = swap(near, far)
        old_by = -back_d / back_r * (inverse_center if at == 1 else 1.0)
        new_by, product_by = 1.0 / back_r, 1.0
        if not last:
            scale_d, scale_r = steps[at]
            new_by, old_by, product_by = scale_d + scale_r * new_by, scale_r * old_by, scale_r
        made = rest(rest_body(1.0, new_by, old_by, product_by, last), near, far, dirn, before, last)
        landing = landed(near_in, far_in)
        before = (dirn,) + before
    (res,) = call(
        last_body,
        (sds(state),),
        (arrived, made[0], landing, table, turned, counts),
        (VM,) + (ANY,) * 4 + (SM,),
        ((state, F32), ((FACE, width), F32), (tables, BF), (turns, BF), (state, F32), (held, F32)),
        8,
        100_000_000,
        CRITICAL_GRANT,
    )
    return (made[1][None, None], res[None, None])


def solution(mesh):
    placed = (
        P("clus", "sub", None, None),
        P("clus", "sub", None, None),
        P("clus", "sub", None, None),
        P("clus", None, None),
        P("clus", None),
        P("clus", "sub", None),
    )
    return jax.shard_map(
        on_device,
        mesh=mesh,
        in_specs=placed,
        out_specs=(P("clus", "sub", None, None), P("clus", "sub", None, None)),
        check_vma=False,
    )
```

```python
import jax
import jax.numpy as jnp
from jax import lax
from jax.experimental import pallas as pl
from jax.experimental.pallas import tpu as pltpu
from jax.sharding import PartitionSpec as P

LOC = 896
NCOR = 24
NPAD = 32
XC = 128
FACE = 2 * XC
CAP = 16
SUBS = 16
MID = SUBS * CAP
BORDER = FACE + MID
SPAN = CAP + 8
ITERS = 3
COARSE = SUBS * NCOR
ROWS = CAP + NCOR
WIDE = 256

spectrum_low = 0.5
spectrum_high = 3.0
center_value = (spectrum_high + spectrum_low) / 2.0
half_width = (spectrum_high - spectrum_low) / 2.0
sigma_one = center_value / half_width

WINDOW_GRANT, CRITICAL_GRANT, FIRST_GRANT = 52, 51, 59
BF = jnp.bfloat16
F32 = jnp.float32
SM = pl.BlockSpec(memory_space=pltpu.SMEM)
ANY = pl.BlockSpec(memory_space=pl.ANY)
VM = pl.BlockSpec(memory_space=pltpu.VMEM)


def split(x):
    hi = x.astype(BF)
    return hi, (x - hi.astype(F32)).astype(BF)


def mm(a, b):
    return jnp.dot(a, b, preferred_element_type=F32)


def mm3(ahi, alo, bhi, blo):
    return mm(ahi, bhi) + (mm(ahi, blo) + mm(alo, bhi))


def sds(shape, dtype=F32):
    return jax.ShapeDtypeStruct(shape, dtype)


def call(body, outs, ins, specs, scratch, copies, flops, grant=WINDOW_GRANT):
    return pl.pallas_call(
        body,
        out_shape=outs,
        in_specs=specs,
        out_specs=tuple(ANY for _ in outs),
        scratch_shapes=tuple(pltpu.VMEM(*s) for s in scratch) + (pltpu.SemaphoreType.DMA((copies,)),),
        compiler_params=pltpu.CompilerParams(vmem_limit_bytes=grant * 1024 * 1024),
        cost_estimate=pl.CostEstimate(flops=flops, bytes_accessed=6_000_000, transcendentals=0),
    )(*ins)


class Copies:
    def __init__(self, sems):
        self.sems, self.used, self.open = sems, 0, []

    def get(self, source, target):
        copy = pltpu.make_async_copy(source, target, self.sems.at[self.used])
        self.used += 1
        copy.start()
        return copy

    def put(self, source, target):
        self.open.append(self.get(source, target))

    def finish(self):
        for copy in self.open:
            copy.wait()


def face_starts(counts):
    starts, at = [], 0
    for p in range(SUBS):
        starts.append(at)
        at = at + counts[0, p]
    return starts, at


def place(at):
    low = lax.rem(at, 8)
    return pl.ds(pl.multiple_of(at - low, 8), SPAN), low


def take_rows(source, at):
    if isinstance(at, int):
        return source[at : at + CAP]
    window, low = place(at)
    return pltpu.roll(source[window, :], lax.rem(SPAN - low, SPAN), 0)[:CAP]


def put_rows(target, at, rows):
    if isinstance(at, int):
        target[at : at + CAP] = rows
        return
    window, low = place(at)
    moved = pltpu.roll(jnp.concatenate([rows, rows[:8]], axis=0), low, 0)
    keep = lax.broadcasted_iota(jnp.int32, moved.shape, 0) >= low
    target[window, :] = jnp.where(keep, moved, target[window, :])


def columns(width):
    return [pl.ds(at, WIDE) for at in range(0, width, WIDE)]


def fill(out, cols, product):
    for p in range(SUBS):
        out[p, :CAP, cols] = product[p * CAP : (p + 1) * CAP]
        out[p, CAP:, cols] = product[MID : MID + NCOR]


def padded(basis):
    return jnp.concatenate([basis, jnp.zeros((NPAD - NCOR, basis.shape[1]), F32)], axis=0)


def even_cluster():
    return lax.rem(lax.axis_index("clus"), 2) == 0


def pick(near, far):
    even = even_cluster()
    return jnp.where(even, far, near), jnp.where(even, near, far)


def first_body(rhs, op, basis, counts, out, mhe, mle, mhr, mlr, rhs_v, held, basis_v, out_v, mhi_v, mlo_v, sems):
    flow = Copies(sems)
    rows_in = flow.get(op.at[pl.ds(FACE, MID + 8)], held)
    basis_in = flow.get(basis, basis_v)
    blocks = columns(rhs.shape[1])
    rhs_in = [flow.get(rhs.at[:, cols], rhs_v.at[:, cols]) for cols in blocks]
    basis_in.wait()
    mhi_v[MID:], mlo_v[MID:] = split(padded(basis_v[...]))
    starts, _ = face_starts(counts)
    rows_in.wait()
    for p in range(SUBS):
        rows = slice(p * CAP, (p + 1) * CAP)
        mhi_v[rows], mlo_v[rows] = split(take_rows(held, starts[p]))
    for source, near_face, others in ((mhi_v, mhe, mhr), (mlo_v, mle, mlr)):
        flow.put(source.at[:, pl.ds(0, BORDER)], near_face)
        flow.put(source.at[:, pl.ds(BORDER, LOC - BORDER)], others)
    for cols, ready in zip(blocks, rhs_in):
        ready.wait()
        dhi, dlo = split(rhs_v[:, cols] * (1.0 / center_value))
        fill(out_v, cols, mm3(mhi_v[...], mlo_v[...], dhi, dlo))
        flow.put(out_v.at[:, :, cols], out.at[:, :, cols])
    flow.finish()


def edge_rows(flow, blocks, ends, direction, near, far, near_v, far_v):
    for at, cols in enumerate(blocks):
        dhi, dlo = split(direction(at, cols))
        if at == 0:
            zhi, zlo = split(ends())
        product = mm3(zhi, zlo, dhi, dlo)
        far_v[:, cols], near_v[:, cols] = pick(product[XC:], product[:XC])
        flow.put(far_v.at[:, cols], far.at[:, cols])
        flow.put(near_v.at[:, cols], near.at[:, cols])
    flow.finish()


def edge_first_body(rhs, op, near, far, rhs_v, ends_v, near_v, far_v, sems):
    flow = Copies(sems)
    blocks = columns(rhs.shape[1])
    ends_in = flow.get(op.at[pl.ds(0, FACE)], ends_v)
    rhs_in = [flow.get(rhs.at[:, cols], rhs_v.at[:, cols]) for cols in blocks]

    def ends():
        ends_in.wait()
        return ends_v[...]

    def direction(at, cols):
        rhs_in[at].wait()
        return rhs_v[:, cols] * (1.0 / center_value)

    edge_rows(flow, blocks, ends, direction, near, far, near_v, far_v)


def edge_body(scale_r):
    def body(part, small, base, turned, op, dirn, near, far, part_v, small_v, base_v, turned_v, ends_v, dirn_v, near_v, far_v, sems):
        flow = Copies(sems)
        blocks = columns(base.shape[1])
        first_in = [flow.get(turned, turned_v), flow.get(small, small_v)]
        block_in = [[flow.get(x.at[:, cols], y.at[:, cols]) for x, y in ((part, part_v), (base.at[pl.ds(0, LOC)], base_v))] for cols in blocks]
        ends_in = flow.get(op.at[pl.ds(0, FACE)], ends_v)

        def ends():
            ends_in.wait()
            return ends_v[...]

        def direction(at, cols):
            for copy in (first_in if at == 0 else []) + block_in[at]:
                copy.wait()
            fix = mm(turned_v[...], small_v[:, cols])
            top, rest = slice(0, BORDER), slice(BORDER, LOC)
            dirn_v[top, cols] = base_v[top, cols] + scale_r * (part_v[:, cols] - fix[top])
            dirn_v[rest, cols] = base_v[rest, cols] - scale_r * fix[rest]
            flow.put(dirn_v.at[:, cols], dirn.at[:, cols])
            return dirn_v[:, cols]

        edge_rows(flow, blocks, ends, direction, near, far, near_v, far_v)

    return body


def landed_body(near_in, far_in, edge, sems):
    flow = Copies(sems)
    even = even_cluster()
    near_at = pl.multiple_of(jnp.where(even, XC, 0), XC)
    far_at = pl.multiple_of(jnp.where(even, 0, XC), XC)
    flow.put(near_in, edge.at[pl.ds(near_at, XC)])
    flow.put(far_in, edge.at[pl.ds(far_at, XC)])
    flow.finish()


def table_rows(inverse_v, places, place_v, rows):
    own = lax.axis_index("sub") * NCOR
    rows[NCOR:] = jnp.zeros((NPAD - NCOR, COARSE), F32)
    for n in range(NCOR):
        rows[n : n + 1] = inverse_v[pl.ds(places[0, own + n], 1), :]
    chosen = lax.broadcasted_iota(jnp.int32, (COARSE, COARSE), 0) == place_v[...]
    chosen = jnp.where(chosen, 1.0, 0.0).astype(BF)
    top, mid = split(rows[...])
    low = (rows[...] - top.astype(F32) - mid.astype(F32)).astype(BF)
    return mm(top, chosen) + (mm(mid, chosen) + mm(low, chosen))


def m_copies(flow, parts, mhi_v, mlo_v):
    mhe, mle, mhr, mlr = parts
    top, rest = pl.ds(0, BORDER), pl.ds(BORDER, LOC - BORDER)
    pairs_in = ((mhe, mhi_v.at[:, top]), (mhr, mhi_v.at[:, rest]), (mle, mlo_v.at[:, top]), (mlr, mlo_v.at[:, rest]))
    return [flow.get(source, target) for source, target in pairs_in]


def table_body(inverse, places, place_row, basis, mhe, mle, mhr, mlr, table, turned, crossed, inverse_v, place_v, basis_v, rows, mhi_v, mlo_v, table_v, turned_v, crossed_v, sems):
    flow = Copies(sems)
    inverse_in = [flow.get(inverse, inverse_v), flow.get(place_row, place_v)]
    basis_in = flow.get(basis, basis_v)
    m_in = m_copies(flow, (mhe, mle, mhr, mlr), mhi_v, mlo_v)
    for copy in inverse_in:
        copy.wait()
    table_v[:NPAD], table_v[NPAD:] = split(table_rows(inverse_v, places, place_v, rows))
    flow.put(table_v, table)
    basis_in.wait()
    bhi, blo = split(padded(basis_v[...]).T)
    turned_v[...] = jnp.concatenate([bhi, bhi, blo], axis=1)
    flow.put(turned_v, turned)
    for copy in m_in:
        copy.wait()
    chi, clo = split(mm3(mhi_v[...], mlo_v[...], bhi, blo))
    crossed_v[...] = jnp.concatenate([chi, chi, clo], axis=1)
    flow.put(crossed_v, crossed)
    flow.finish()


AHEAD = pl.ds(LOC, MID + NPAD)
HALF = (LOC - FACE) // 2
CHUNKS = (pl.ds(FACE, HALF), pl.ds(FACE + HALF, HALF))


def rest_body(in_scale, new_by, old_by, product_by, last):
    olds = 0 if old_by is None else 2 if last else 1

    def body(op, near, far, dirn, *refs):
        before, refs = refs[:olds], refs[olds:]
        parts, refs = (refs[:4], refs[4:]) if not last else ((), refs)
        outs, refs = refs[: 1 + last], refs[1 + last :]
        (op_v, near_v, far_v, dirn_v), refs = refs[:4], refs[4:]
        before_v, refs = refs[:olds], refs[olds:]
        m_v, refs = (refs[:2], refs[2:]) if not last else ((), refs)
        made, sems = refs[:-1], refs[-1]
        flow = Copies(sems)
        blocks = columns(dirn.shape[1])
        op_in, dirn_in, before_in, m_in = [], [], [], []
        for at, cols in enumerate(blocks):
            dirn_in.append(flow.get(dirn.at[:, cols], dirn_v.at[:, cols]))
            if at == 0:
                op_in.append(flow.get(op.at[CHUNKS[0]], op_v.at[CHUNKS[0]]))
            before_in.append([flow.get(x.at[:, cols], y.at[:, cols]) for x, y in zip(before, before_v)])
            if at == 0:
                op_in.append(flow.get(op.at[CHUNKS[1]], op_v.at[CHUNKS[1]]))
                edges_in = [flow.get(near, near_v), flow.get(far, far_v)]
                m_in = [] if last else m_copies(flow, parts, *m_v)
        factors = []
        for at, cols in enumerate(blocks):
            dirn_in[at].wait()
            dhi, dlo = split(dirn_v[:, cols] * in_scale)

            def store(rows, product):
                value = new_by * dirn_v[rows, cols] - product_by * product
                if olds:
                    value = value + old_by * before_v[0][rows, cols]
                made[0][rows, cols] = value
                flow.put(made[0].at[rows, cols], outs[0].at[rows, cols])

            for part, rows in enumerate(CHUNKS):
                if at == 0:
                    op_in[part].wait()
                    factors.append(split(op_v[rows]))
                if part == 0:
                    for copy in before_in[at]:
                        copy.wait()
                store(rows, mm3(*factors[part], dhi, dlo))
            if at == 0:
                for copy in edges_in:
                    copy.wait()
            low, high = pick(near_v[:, cols], far_v[:, cols])
            store(pl.ds(0, FACE), jnp.concatenate([low, high], axis=0))
            if last:
                made[1][:, cols] = before_v[1][:, cols] * (1.0 / center_value) + before_v[0][:, cols] + dirn_v[:, cols]
                flow.put(made[1].at[:, cols], outs[1].at[:, cols])
            else:
                if at == 0:
                    for copy in m_in:
                        copy.wait()
                made[1][:, cols] = mm3(m_v[0][...], m_v[1][...], *split(made[0][:, cols]))
                flow.put(made[1].at[:, cols], outs[0].at[AHEAD, cols])
        flow.finish()

    return body


def arrived_faces(cols, arrived, starts, total, inner):
    for p in range(SUBS):
        put_rows(inner, starts[p], arrived[p, :CAP, cols])
    usable = lax.broadcasted_iota(jnp.int32, (MID, WIDE), 0) < total
    return jnp.where(usable, inner[:MID], 0.0)


def arrived_back(cols, arrived, table):
    pieces = jnp.concatenate([arrived[p, CAP:, cols] for p in range(SUBS)], axis=0)
    phi, plo = split(pieces)
    both = mm(table[...], phi)
    back = both[:NPAD] + (both[NPAD:] + mm(table[:NPAD], plo))
    yhi, ylo = split(back)
    return jnp.concatenate([yhi, ylo, yhi], axis=0)


def update(cols, source, edge, fix, faces, scale, store):
    rows = slice(0, FACE)
    store(rows, source[rows, cols] + scale * (edge[:, cols] - fix[rows]))
    rows = slice(FACE, FACE + MID)
    store(rows, source[rows, cols] + scale * (faces - fix[rows]))
    rows = slice(FACE + MID, LOC)
    store(rows, source[rows, cols] - scale * fix[rows])


def next_body(scale_r):
    def body(arrived, mhe, mle, table, crossed, ahead, edge, counts, out, part, small, ahead_v, part_v, small_v, out_v, inner, sems):
        flow = Copies(sems)
        edge_in = flow.get(edge, part_v.at[pl.ds(0, FACE)])
        ahead_in = flow.get(ahead.at[AHEAD], ahead_v)
        starts, total = face_starts(counts)
        blocks = columns(edge.shape[1])
        for cols in blocks:
            small_v[:, cols] = arrived_back(cols, arrived, table)
            part_v[FACE:, cols] = arrived_faces(cols, arrived, starts, total, inner)
        flow.put(small_v, small)
        edge_in.wait()
        flow.put(part_v, part)
        for at, cols in enumerate(blocks):
            product = mm3(mhe[...], mle[...], *split(part_v[:, cols])) - mm(crossed[...], small_v[:, cols])
            if at == 0:
                ahead_in.wait()
            fill(out_v, cols, ahead_v[:, cols] + scale_r * product)
            flow.put(out_v.at[:, :, cols], out.at[:, :, cols])
        flow.finish()

    return body


def last_body(arrived, left, edge, table, turned, counts, res, arrived_v, left_v, edge_v, turned_v, res_v, inner, sems):
    flow = Copies(sems)
    starts, total = face_starts(counts)
    blocks = columns(left.shape[1])
    arrived_in = [flow.get(arrived.at[:, :, cols], arrived_v.at[:, :, cols]) for cols in blocks]
    turned_in = flow.get(turned, turned_v)
    edge_in = flow.get(edge, edge_v)
    left_in = [flow.get(left.at[:, cols], left_v.at[:, cols]) for cols in blocks]
    got = []
    for cols, ready in zip(blocks, arrived_in):
        ready.wait()
        got.append((arrived_faces(cols, arrived_v, starts, total, inner), arrived_back(cols, arrived_v, table)))
    turned_in.wait()
    for at, cols in enumerate(blocks):
        faces, back = got[at]
        fix = mm(turned_v[...], back)
        if at == 0:
            edge_in.wait()
        left_in[at].wait()

        def store(rows, value):
            res_v[rows, cols] = value

        update(cols, left_v, edge_v, fix, faces, 1.0, store)
        flow.put(res_v.at[:, cols], res.at[:, cols])
    flow.finish()


def pairs(first, count):
    route = []
    for low in range(first, count - 1, 2):
        route += [(low, low + 1), (low + 1, low)]
    return route


def scales():
    found, ratio = [], 1.0 / sigma_one
    for _ in range(ITERS - 1):
        ratio_next = 1.0 / (2.0 * sigma_one - ratio)
        found.append((ratio_next * ratio, 2.0 * ratio_next / half_width))
        ratio = ratio_next
    return found


def on_device(right_side, dual_operator, corner_basis, coarse_inverse, corner_map, iface_counts):
    rhs = right_side[0, 0]
    op = dual_operator[0, 0]
    basis = corner_basis[0, 0]
    inverse = coarse_inverse[0]
    counts = iface_counts[0]
    width = rhs.shape[1]
    clusters = lax.axis_size("clus")
    state, edge, sent = (LOC, width), (XC, width), (SUBS, ROWS, width)
    mids, ends = (MID + NPAD, LOC), (FACE, LOC)
    tables, turns, held = (2 * NPAD, COARSE), (LOC, 3 * NPAD), (MID + 8, WIDE)
    steps = scales()

    def exchange(out):
        return lax.all_to_all(out, "sub", split_axis=0, concat_axis=0, tiled=True)

    def swap(near, far):
        far = lax.ppermute(far, "clus", pairs(1, clusters))
        return lax.ppermute(near, "clus", pairs(0, clusters)), far

    def landed(near_in, far_in):
        return call(landed_body, (sds((FACE, width)),), (near_in, far_in), (VM, VM), (), 2, 1_000_000, WINDOW_GRANT)[0]

    border, others = (MID + NPAD, BORDER), (MID + NPAD, LOC - BORDER)
    crosses, ahead_s, part_s, small_s = (MID + NPAD, 3 * NPAD), (MID + NPAD, width), (BORDER, width), (3 * NPAD, width)
    inverse_center = 1.0 / center_value

    out, mhe, mle, mhr, mlr = call(
        first_body,
        (sds(sent), sds(border, BF), sds(border, BF), sds(others, BF), sds(others, BF)),
        (rhs, op, basis, counts),
        (ANY, ANY, ANY, SM),
        ((state, F32), ((MID + 8, LOC), F32), ((NCOR, LOC), F32), (sent, F32), (mids, BF), (mids, BF)),
        10,
        800_000_000,
        FIRST_GRANT,
    )
    parts = (mhe, mle, mhr, mlr)

    def rest(body, near, far, dirn, before, last):
        return call(
            body,
            (sds(state), sds(state)) if last else (sds((LOC + MID + NPAD, width)),),
            (op, near, far, dirn) + before + (() if last else parts),
            (ANY,) * (4 + len(before) + 4 * (not last)),
            (((LOC, LOC), F32), (edge, F32), (edge, F32), (state, F32)) + ((state, F32),) * len(before)
            + (() if last else ((mids, BF), (mids, BF))) + ((state, F32), (state if last else ahead_s, F32)),
            24,
            2_000_000_000,
            WINDOW_GRANT,
        )

    arrived = exchange(out)
    near, far = call(
        edge_first_body,
        (sds(edge), sds(edge)),
        (rhs, op),
        (ANY, ANY),
        ((state, F32), (ends, F32), (edge, F32), (edge, F32)),
        7,
        700_000_000,
    )
    near_in, far_in = swap(near, far)
    scale_d, scale_r = steps[0]
    made = rest(rest_body(inverse_center, scale_d * inverse_center + scale_r, None, scale_r, False), near, far, rhs, (), False)
    table, turned, crossed = call(
        table_body,
        (sds(tables, BF), sds(turns, BF), sds(crosses, BF)),
        (inverse, corner_map, corner_map, basis) + parts,
        (ANY, SM) + (ANY,) * 6,
        (((COARSE, COARSE), F32), ((1, COARSE), jnp.int32), ((NCOR, LOC), F32), ((NPAD, COARSE), F32), (mids, BF), (mids, BF),
         (tables, BF), (turns, BF), (crosses, BF)),
        10,
        200_000_000,
        WINDOW_GRANT,
    )
    landing = landed(near_in, far_in)
    before = (rhs,)
    for at in range(1, ITERS):
        last = at == ITERS - 1
        back_d, back_r = steps[at - 1]
        out, part, small = call(
            next_body(back_r),
            (sds(sent), sds(part_s), sds(small_s, BF)),
            (arrived, mhe, mle, table, crossed, made[0], landing, counts),
            (VM,) * 5 + (ANY,) * 2 + (SM,),
            ((ahead_s, F32), (part_s, F32), (small_s, BF), (sent, F32), (held, F32)),
            7,
            1_000_000_000,
            CRITICAL_GRANT,
        )
        arrived = exchange(out)
        dirn, near, far = call(
            edge_body(back_r),
            (sds(state), sds(edge), sds(edge)),
            (part, small, made[0], turned, op),
            (ANY,) * 5,
            ((part_s, F32), (small_s, BF), (state, F32), (turns, BF), (ends, F32), (state, F32), (edge, F32), (edge, F32)),
            13,
            700_000_000,
        )
        near_in, far_in = swap(near, far)
        old_by = -back_d / back_r * (inverse_center if at == 1 else 1.0)
        new_by, product_by = 1.0 / back_r, 1.0
        if not last:
            scale_d, scale_r = steps[at]
            new_by, old_by, product_by = scale_d + scale_r * new_by, scale_r * old_by, scale_r
        made = rest(rest_body(1.0, new_by, old_by, product_by, last), near, far, dirn, before, last)
        landing = landed(near_in, far_in)
        before = (dirn,) + before
    (res,) = call(
        last_body,
        (sds(state),),
        (arrived, made[0], landing, table, turned, counts),
        (ANY, ANY, ANY, VM, ANY, SM),
        ((sent, F32), (state, F32), ((FACE, width), F32), (turns, BF), (state, F32), (held, F32)),
        8,
        100_000_000,
        CRITICAL_GRANT,
    )
    return (made[1][None, None], res[None, None])


def solution(mesh):
    placed = (
        P("clus", "sub", None, None),
        P("clus", "sub", None, None),
        P("clus", "sub", None, None),
        P("clus", None, None),
        P("clus", None),
        P("clus", "sub", None),
    )
    return jax.shard_map(
        on_device,
        mesh=mesh,
        in_specs=placed,
        out_specs=(P("clus", "sub", None, None), P("clus", "sub", None, None)),
        check_vma=False,
    )
```

```python
import jax
import jax.numpy as jnp
from jax import lax
from jax.experimental import pallas as pl
from jax.experimental.pallas import tpu as pltpu
from jax.sharding import PartitionSpec as P

LOC = 896
NCOR = 24
NPAD = 32
XC = 128
FACE = 2 * XC
CAP = 16
SUBS = 16
MID = SUBS * CAP
BORDER = FACE + MID
SPAN = CAP + 8
ITERS = 3
COARSE = SUBS * NCOR
ROWS = CAP + NCOR
WIDE = 256

spectrum_low = 0.5
spectrum_high = 3.0
center_value = (spectrum_high + spectrum_low) / 2.0
half_width = (spectrum_high - spectrum_low) / 2.0
sigma_one = center_value / half_width

WINDOW_GRANT, CRITICAL_GRANT, FIRST_GRANT = 52, 51, 59
BF = jnp.bfloat16
F32 = jnp.float32
SM = pl.BlockSpec(memory_space=pltpu.SMEM)
ANY = pl.BlockSpec(memory_space=pl.ANY)
VM = pl.BlockSpec(memory_space=pltpu.VMEM)


def split(x):
    hi = x.astype(BF)
    return hi, (x - hi.astype(F32)).astype(BF)


def mm(a, b):
    return jnp.dot(a, b, preferred_element_type=F32)


def mm3(ahi, alo, bhi, blo):
    return mm(ahi, bhi) + (mm(ahi, blo) + mm(alo, bhi))


def sds(shape, dtype=F32):
    return jax.ShapeDtypeStruct(shape, dtype)


def call(body, outs, ins, specs, scratch, copies, flops, grant=WINDOW_GRANT):
    return pl.pallas_call(
        body,
        out_shape=outs,
        in_specs=specs,
        out_specs=tuple(ANY for _ in outs),
        scratch_shapes=tuple(pltpu.VMEM(*s) for s in scratch) + (pltpu.SemaphoreType.DMA((copies,)),),
        compiler_params=pltpu.CompilerParams(vmem_limit_bytes=grant * 1024 * 1024),
        cost_estimate=pl.CostEstimate(flops=flops, bytes_accessed=6_000_000, transcendentals=0),
    )(*ins)


class Copies:
    def __init__(self, sems):
        self.sems, self.used, self.open = sems, 0, []

    def get(self, source, target):
        copy = pltpu.make_async_copy(source, target, self.sems.at[self.used])
        self.used += 1
        copy.start()
        return copy

    def put(self, source, target):
        self.open.append(self.get(source, target))

    def finish(self):
        for copy in self.open:
            copy.wait()


def face_starts(counts):
    starts, at = [], 0
    for p in range(SUBS):
        starts.append(at)
        at = at + counts[0, p]
    return starts, at


def place(at):
    low = lax.rem(at, 8)
    return pl.ds(pl.multiple_of(at - low, 8), SPAN), low


def take_rows(source, at):
    if isinstance(at, int):
        return source[at : at + CAP]
    window, low = place(at)
    return pltpu.roll(source[window, :], lax.rem(SPAN - low, SPAN), 0)[:CAP]


def put_rows(target, at, rows):
    if isinstance(at, int):
        target[at : at + CAP] = rows
        return
    window, low = place(at)
    moved = pltpu.roll(jnp.concatenate([rows, rows[:8]], axis=0), low, 0)
    keep = lax.broadcasted_iota(jnp.int32, moved.shape, 0) >= low
    target[window, :] = jnp.where(keep, moved, target[window, :])


def columns(width):
    return [pl.ds(at, WIDE) for at in range(0, width, WIDE)]


def fill(out, cols, product):
    for p in range(SUBS):
        out[p, :CAP, cols] = product[p * CAP : (p + 1) * CAP]
        out[p, CAP:, cols] = product[MID : MID + NCOR]


def padded(basis):
    return jnp.concatenate([basis, jnp.zeros((NPAD - NCOR, basis.shape[1]), F32)], axis=0)


def even_cluster():
    return lax.rem(lax.axis_index("clus"), 2) == 0


def pick(near, far):
    even = even_cluster()
    return jnp.where(even, far, near), jnp.where(even, near, far)


def first_body(rhs, op, basis, counts, out, mhe, mle, mhr, mlr, rhs_v, held, basis_v, out_v, mhi_v, mlo_v, sems):
    flow = Copies(sems)
    rows_in = flow.get(op.at[pl.ds(FACE, MID + 8)], held)
    basis_in = flow.get(basis, basis_v)
    blocks = columns(rhs.shape[1])
    rhs_in = [flow.get(rhs.at[:, cols], rhs_v.at[:, cols]) for cols in blocks]
    basis_in.wait()
    mhi_v[MID:], mlo_v[MID:] = split(padded(basis_v[...]))
    starts, _ = face_starts(counts)
    rows_in.wait()
    for p in range(SUBS):
        rows = slice(p * CAP, (p + 1) * CAP)
        mhi_v[rows], mlo_v[rows] = split(take_rows(held, starts[p]))
    for source, near_face, others in ((mhi_v, mhe, mhr), (mlo_v, mle, mlr)):
        flow.put(source.at[:, pl.ds(0, BORDER)], near_face)
        flow.put(source.at[:, pl.ds(BORDER, LOC - BORDER)], others)
    for cols, ready in zip(blocks, rhs_in):
        ready.wait()
        dhi, dlo = split(rhs_v[:, cols] * (1.0 / center_value))
        fill(out_v, cols, mm3(mhi_v[...], mlo_v[...], dhi, dlo))
        flow.put(out_v.at[:, :, cols], out.at[:, :, cols])
    flow.finish()


def edge_rows(flow, blocks, ends, direction, near, far, near_v, far_v):
    for at, cols in enumerate(blocks):
        dhi, dlo = split(direction(at, cols))
        if at == 0:
            zhi, zlo = split(ends())
        product = mm3(zhi, zlo, dhi, dlo)
        far_v[:, cols], near_v[:, cols] = pick(product[XC:], product[:XC])
        flow.put(far_v.at[:, cols], far.at[:, cols])
        flow.put(near_v.at[:, cols], near.at[:, cols])
    flow.finish()


def edge_first_body(rhs, op, near, far, rhs_v, ends_v, near_v, far_v, sems):
    flow = Copies(sems)
    blocks = columns(rhs.shape[1])
    ends_in = flow.get(op.at[pl.ds(0, FACE)], ends_v)
    rhs_in = [flow.get(rhs.at[:, cols], rhs_v.at[:, cols]) for cols in blocks]

    def ends():
        ends_in.wait()
        return ends_v[...]

    def direction(at, cols):
        rhs_in[at].wait()
        return rhs_v[:, cols] * (1.0 / center_value)

    edge_rows(flow, blocks, ends, direction, near, far, near_v, far_v)


def edge_body(scale_r):
    def body(part, small, base, turned, op, dirn, near, far, part_v, small_v, base_v, turned_v, ends_v, dirn_v, near_v, far_v, sems):
        flow = Copies(sems)
        blocks = columns(base.shape[1])
        first_in = [flow.get(turned, turned_v), flow.get(small, small_v)]
        block_in = [[flow.get(x.at[:, cols], y.at[:, cols]) for x, y in ((part, part_v), (base.at[pl.ds(0, LOC)], base_v))] for cols in blocks]
        ends_in = flow.get(op.at[pl.ds(0, FACE)], ends_v)

        def ends():
            ends_in.wait()
            return ends_v[...]

        def direction(at, cols):
            for copy in (first_in if at == 0 else []) + block_in[at]:
                copy.wait()
            fix = mm(turned_v[...], small_v[:, cols])
            top, rest = slice(0, BORDER), slice(BORDER, LOC)
            dirn_v[top, cols] = base_v[top, cols] + scale_r * (part_v[:, cols] - fix[top])
            dirn_v[rest, cols] = base_v[rest, cols] - scale_r * fix[rest]
            flow.put(dirn_v.at[:, cols], dirn.at[:, cols])
            return dirn_v[:, cols]

        edge_rows(flow, blocks, ends, direction, near, far, near_v, far_v)

    return body


def landed_body(near_in, far_in, edge, sems):
    flow = Copies(sems)
    even = even_cluster()
    near_at = pl.multiple_of(jnp.where(even, XC, 0), XC)
    far_at = pl.multiple_of(jnp.where(even, 0, XC), XC)
    flow.put(near_in, edge.at[pl.ds(near_at, XC)])
    flow.put(far_in, edge.at[pl.ds(far_at, XC)])
    flow.finish()


def table_rows(inverse_v, places, place_v, rows):
    own = lax.axis_index("sub") * NCOR
    rows[NCOR:] = jnp.zeros((NPAD - NCOR, COARSE), F32)
    for n in range(NCOR):
        rows[n : n + 1] = inverse_v[pl.ds(places[0, own + n], 1), :]
    chosen = lax.broadcasted_iota(jnp.int32, (COARSE, COARSE), 0) == place_v[...]
    chosen = jnp.where(chosen, 1.0, 0.0).astype(BF)
    top, mid = split(rows[...])
    low = (rows[...] - top.astype(F32) - mid.astype(F32)).astype(BF)
    return mm(top, chosen) + (mm(mid, chosen) + mm(low, chosen))


def m_copies(flow, parts, mhi_v, mlo_v):
    mhe, mle, mhr, mlr = parts
    top, rest = pl.ds(0, BORDER), pl.ds(BORDER, LOC - BORDER)
    pairs_in = ((mhe, mhi_v.at[:, top]), (mhr, mhi_v.at[:, rest]), (mle, mlo_v.at[:, top]), (mlr, mlo_v.at[:, rest]))
    return [flow.get(source, target) for source, target in pairs_in]


def table_body(inverse, places, place_row, basis, mhe, mle, mhr, mlr, table, turned, crossed, inverse_v, place_v, basis_v, rows, mhi_v, mlo_v, table_v, turned_v, crossed_v, sems):
    flow = Copies(sems)
    inverse_in = [flow.get(inverse, inverse_v), flow.get(place_row, place_v)]
    basis_in = flow.get(basis, basis_v)
    m_in = m_copies(flow, (mhe, mle, mhr, mlr), mhi_v, mlo_v)
    for copy in inverse_in:
        copy.wait()
    table_v[:NPAD], table_v[NPAD:] = split(table_rows(inverse_v, places, place_v, rows))
    flow.put(table_v, table)
    basis_in.wait()
    bhi, blo = split(padded(basis_v[...]).T)
    turned_v[...] = jnp.concatenate([bhi, bhi, blo], axis=1)
    flow.put(turned_v, turned)
    for copy in m_in:
        copy.wait()
    chi, clo = split(mm3(mhi_v[...], mlo_v[...], bhi, blo))
    crossed_v[...] = jnp.concatenate([chi, chi, clo], axis=1)
    flow.put(crossed_v, crossed)
    flow.finish()


AHEAD = pl.ds(LOC, MID + NPAD)
HALF = (LOC - FACE) // 2
CHUNKS = (pl.ds(FACE, HALF), pl.ds(FACE + HALF, HALF))


def rest_body(in_scale, new_by, old_by, product_by, last):
    olds = 0 if old_by is None else 2 if last else 1

    def body(op, near, far, dirn, *refs):
        before, refs = refs[:olds], refs[olds:]
        parts, refs = (refs[:4], refs[4:]) if not last else ((), refs)
        outs, refs = refs[: 1 + last], refs[1 + last :]
        (op_v, dirn_v), refs = refs[:2], refs[2:]
        before_v, refs = refs[:olds], refs[olds:]
        made, sems = refs[:-1], refs[-1]
        flow = Copies(sems)
        blocks = columns(dirn.shape[1])
        op_in, dirn_in, before_in = [], [], []
        for at, cols in enumerate(blocks):
            dirn_in.append(flow.get(dirn.at[:, cols], dirn_v.at[:, cols]))
            if at == 0:
                op_in.append(flow.get(op.at[CHUNKS[0]], op_v.at[CHUNKS[0]]))
            before_in.append([flow.get(x.at[:, cols], y.at[:, cols]) for x, y in zip(before, before_v)])
            if at == 0:
                op_in.append(flow.get(op.at[CHUNKS[1]], op_v.at[CHUNKS[1]]))
        factors = []
        for at, cols in enumerate(blocks):
            dirn_in[at].wait()
            dhi, dlo = split(dirn_v[:, cols] * in_scale)

            def store(rows, product):
                value = new_by * dirn_v[rows, cols] - product_by * product
                if olds:
                    value = value + old_by * before_v[0][rows, cols]
                made[0][rows, cols] = value
                flow.put(made[0].at[rows, cols], outs[0].at[rows, cols])

            for part, rows in enumerate(CHUNKS):
                if at == 0:
                    op_in[part].wait()
                    factors.append(split(op_v[rows]))
                if part == 0:
                    for copy in before_in[at]:
                        copy.wait()
                store(rows, mm3(*factors[part], dhi, dlo))
            low, high = pick(near[:, cols], far[:, cols])
            store(pl.ds(0, FACE), jnp.concatenate([low, high], axis=0))
            if last:
                made[1][:, cols] = before_v[1][:, cols] * (1.0 / center_value) + before_v[0][:, cols] + dirn_v[:, cols]
                flow.put(made[1].at[:, cols], outs[1].at[:, cols])
            else:
                mhe, mle, mhr, mlr = parts
                bhi, blo = split(made[0][:, cols])
                product = mm3(mhe[...], mle[...], bhi[:BORDER], blo[:BORDER])
                made[1][:, cols] = product + mm3(mhr[...], mlr[...], bhi[BORDER:], blo[BORDER:])
                flow.put(made[1].at[:, cols], outs[0].at[AHEAD, cols])
        flow.finish()

    return body


def arrived_faces(cols, arrived, starts, total, inner):
    for p in range(SUBS):
        put_rows(inner, starts[p], arrived[p, :CAP, cols])
    usable = lax.broadcasted_iota(jnp.int32, (MID, WIDE), 0) < total
    return jnp.where(usable, inner[:MID], 0.0)


def arrived_back(cols, arrived, table):
    pieces = jnp.concatenate([arrived[p, CAP:, cols] for p in range(SUBS)], axis=0)
    phi, plo = split(pieces)
    both = mm(table[...], phi)
    back = both[:NPAD] + (both[NPAD:] + mm(table[:NPAD], plo))
    yhi, ylo = split(back)
    return jnp.concatenate([yhi, ylo, yhi], axis=0)


def update(cols, source, edge, fix, faces, scale, store):
    rows = slice(0, FACE)
    store(rows, source[rows, cols] + scale * (edge[:, cols] - fix[rows]))
    rows = slice(FACE, FACE + MID)
    store(rows, source[rows, cols] + scale * (faces - fix[rows]))
    rows = slice(FACE + MID, LOC)
    store(rows, source[rows, cols] - scale * fix[rows])


def next_body(scale_r):
    def body(arrived, mhe, mle, table, crossed, ahead, edge, counts, out, part, small, ahead_v, part_v, small_v, out_v, inner, sems):
        flow = Copies(sems)
        edge_in = flow.get(edge, part_v.at[pl.ds(0, FACE)])
        ahead_in = flow.get(ahead.at[AHEAD], ahead_v)
        starts, total = face_starts(counts)
        blocks = columns(edge.shape[1])
        for cols in blocks:
            small_v[:, cols] = arrived_back(cols, arrived, table)
            part_v[FACE:, cols] = arrived_faces(cols, arrived, starts, total, inner)
        flow.put(small_v, small)
        edge_in.wait()
        flow.put(part_v, part)
        for at, cols in enumerate(blocks):
            product = mm3(mhe[...], mle[...], *split(part_v[:, cols])) - mm(crossed[...], small_v[:, cols])
            if at == 0:
                ahead_in.wait()
            fill(out_v, cols, ahead_v[:, cols] + scale_r * product)
            flow.put(out_v.at[:, :, cols], out.at[:, :, cols])
        flow.finish()

    return body


def last_body(arrived, left, edge, table, turned, counts, res, arrived_v, left_v, edge_v, turned_v, res_v, inner, sems):
    flow = Copies(sems)
    starts, total = face_starts(counts)
    blocks = columns(left.shape[1])
    arrived_in = [flow.get(arrived.at[:, :, cols], arrived_v.at[:, :, cols]) for cols in blocks]
    turned_in = flow.get(turned, turned_v)
    edge_in = flow.get(edge, edge_v)
    left_in = [flow.get(left.at[:, cols], left_v.at[:, cols]) for cols in blocks]
    got = []
    for cols, ready in zip(blocks, arrived_in):
        ready.wait()
        got.append((arrived_faces(cols, arrived_v, starts, total, inner), arrived_back(cols, arrived_v, table)))
    turned_in.wait()
    for at, cols in enumerate(blocks):
        faces, back = got[at]
        fix = mm(turned_v[...], back)
        if at == 0:
            edge_in.wait()
        left_in[at].wait()

        def store(rows, value):
            res_v[rows, cols] = value

        update(cols, left_v, edge_v, fix, faces, 1.0, store)
        flow.put(res_v.at[:, cols], res.at[:, cols])
    flow.finish()


def pairs(first, count):
    route = []
    for low in range(first, count - 1, 2):
        route += [(low, low + 1), (low + 1, low)]
    return route


def scales():
    found, ratio = [], 1.0 / sigma_one
    for _ in range(ITERS - 1):
        ratio_next = 1.0 / (2.0 * sigma_one - ratio)
        found.append((ratio_next * ratio, 2.0 * ratio_next / half_width))
        ratio = ratio_next
    return found


def on_device(right_side, dual_operator, corner_basis, coarse_inverse, corner_map, iface_counts):
    rhs = right_side[0, 0]
    op = dual_operator[0, 0]
    basis = corner_basis[0, 0]
    inverse = coarse_inverse[0]
    counts = iface_counts[0]
    width = rhs.shape[1]
    clusters = lax.axis_size("clus")
    state, edge, sent = (LOC, width), (XC, width), (SUBS, ROWS, width)
    mids, ends = (MID + NPAD, LOC), (FACE, LOC)
    tables, turns, held = (2 * NPAD, COARSE), (LOC, 3 * NPAD), (MID + 8, WIDE)
    steps = scales()

    def exchange(out):
        return lax.all_to_all(out, "sub", split_axis=0, concat_axis=0, tiled=True)

    def swap(near, far):
        far = lax.ppermute(far, "clus", pairs(1, clusters))
        return lax.ppermute(near, "clus", pairs(0, clusters)), far

    def landed(near_in, far_in):
        return call(landed_body, (sds((FACE, width)),), (near_in, far_in), (VM, VM), (), 2, 1_000_000, WINDOW_GRANT)[0]

    border, others = (MID + NPAD, BORDER), (MID + NPAD, LOC - BORDER)
    crosses, ahead_s, part_s, small_s = (MID + NPAD, 3 * NPAD), (MID + NPAD, width), (BORDER, width), (3 * NPAD, width)
    inverse_center = 1.0 / center_value

    out, mhe, mle, mhr, mlr = call(
        first_body,
        (sds(sent), sds(border, BF), sds(border, BF), sds(others, BF), sds(others, BF)),
        (rhs, op, basis, counts),
        (ANY, ANY, ANY, SM),
        ((state, F32), ((MID + 8, LOC), F32), ((NCOR, LOC), F32), (sent, F32), (mids, BF), (mids, BF)),
        10,
        800_000_000,
        FIRST_GRANT,
    )
    parts = (mhe, mle, mhr, mlr)

    def rest(body, near, far, dirn, before, last):
        return call(
            body,
            (sds(state), sds(state)) if last else (sds((LOC + MID + NPAD, width)),),
            (op, near, far, dirn) + before + (() if last else parts),
            (ANY, VM, VM, ANY) + (ANY,) * len(before) + (VM,) * (4 * (not last)),
            (((LOC, LOC), F32), (state, F32)) + ((state, F32),) * len(before) + ((state, F32), (state if last else ahead_s, F32)),
            24,
            2_000_000_000,
            WINDOW_GRANT,
        )

    arrived = exchange(out)
    near, far = call(
        edge_first_body,
        (sds(edge), sds(edge)),
        (rhs, op),
        (ANY, ANY),
        ((state, F32), (ends, F32), (edge, F32), (edge, F32)),
        7,
        700_000_000,
    )
    near_in, far_in = swap(near, far)
    scale_d, scale_r = steps[0]
    made = rest(rest_body(inverse_center, scale_d * inverse_center + scale_r, None, scale_r, False), near, far, rhs, (), False)
    table, turned, crossed = call(
        table_body,
        (sds(tables, BF), sds(turns, BF), sds(crosses, BF)),
        (inverse, corner_map, corner_map, basis) + parts,
        (ANY, SM) + (ANY,) * 6,
        (((COARSE, COARSE), F32), ((1, COARSE), jnp.int32), ((NCOR, LOC), F32), ((NPAD, COARSE), F32), (mids, BF), (mids, BF),
         (tables, BF), (turns, BF), (crosses, BF)),
        10,
        200_000_000,
        WINDOW_GRANT,
    )
    landing = landed(near_in, far_in)
    before = (rhs,)
    for at in range(1, ITERS):
        last = at == ITERS - 1
        back_d, back_r = steps[at - 1]
        out, part, small = call(
            next_body(back_r),
            (sds(sent), sds(part_s), sds(small_s, BF)),
            (arrived, mhe, mle, table, crossed, made[0], landing, counts),
            (VM,) * 5 + (ANY,) * 2 + (SM,),
            ((ahead_s, F32), (part_s, F32), (small_s, BF), (sent, F32), (held, F32)),
            7,
            1_000_000_000,
            CRITICAL_GRANT,
        )
        arrived = exchange(out)
        dirn, near, far = call(
            edge_body(back_r),
            (sds(state), sds(edge), sds(edge)),
            (part, small, made[0], turned, op),
            (ANY,) * 5,
            ((part_s, F32), (small_s, BF), (state, F32), (turns, BF), (ends, F32), (state, F32), (edge, F32), (edge, F32)),
            13,
            700_000_000,
        )
        near_in, far_in = swap(near, far)
        old_by = -back_d / back_r * (inverse_center if at == 1 else 1.0)
        new_by, product_by = 1.0 / back_r, 1.0
        if not last:
            scale_d, scale_r = steps[at]
            new_by, old_by, product_by = scale_d + scale_r * new_by, scale_r * old_by, scale_r
        made = rest(rest_body(1.0, new_by, old_by, product_by, last), near, far, dirn, before, last)
        landing = landed(near_in, far_in)
        before = (dirn,) + before
    (res,) = call(
        last_body,
        (sds(state),),
        (arrived, made[0], landing, table, turned, counts),
        (ANY, ANY, ANY, VM, ANY, SM),
        ((sent, F32), (state, F32), ((FACE, width), F32), (turns, BF), (state, F32), (held, F32)),
        8,
        100_000_000,
        CRITICAL_GRANT,
    )
    return (made[1][None, None], res[None, None])


def solution(mesh):
    placed = (
        P("clus", "sub", None, None),
        P("clus", "sub", None, None),
        P("clus", "sub", None, None),
        P("clus", None, None),
        P("clus", None),
        P("clus", "sub", None),
    )
    return jax.shard_map(
        on_device,
        mesh=mesh,
        in_specs=placed,
        out_specs=(P("clus", "sub", None, None), P("clus", "sub", None, None)),
        check_vma=False,
    )
```
